512 devices in a mesh: pts: 128 (over y, z, core), grp: 4 (over x).
Axes of the slice: x: 4, y: 8, z: 8, core: 2. Of those that a mesh axis runs over, the one named last changes fastest.
Arguments:
- jacobian: bfloat16 [65536, 3, 3, 384], P(('pts', 'grp')), may hold values from -0.15625 to 0.15625
- owner: int32 [65536, 1], P(('pts', 'grp')), may hold values from 0 to 127; in each aligned block of 128 rows (0 to 127, 128 to 255, ...) at most 2 rows name the same one
- damping: float32 [128, 384], P('pts'), may hold values from 0.2 to 2
Outputs:
- reduced_diag: float32 [128, 384, 384], P('pts', None, 'grp')
- reduced_pair: float32 [128, 384, 384], P('pts', None, 'grp')
The draws below stay inside these ranges and needn't reach their ends.
Inputs may be any that keep to these rules, and one draw needn't show every extreme that they name: `owner`: among the 128 landmarks of one device at most 2 name the same segment, and in every draw some segment is named by exactly 2 landmarks of some device.
All inputs are finite; a program needn't handle non-finite values.
Results may differ from the reference program's by a relative error of at most 0.0003.
Values may be sent and summed in bfloat16 or wider, within the bound.
No kernel may reach another device: no remote copies, remote signals or barrier semaphores. Data moves between devices by JAX's collectives and lax.ppermute only.
A program may use at most 64 MiB of HBM per device.

```python
import math
import jax
import jax.numpy as jnp
import numpy as np
from jax import lax

F = 384
PT = 128
CAP = 2
NE = 128
NPOINTS = 65536
N_PTS = 128
N_GRP = 4


def level_of(key, dims, cuts, low, top_value):
    def one(position, parts):
        steps = jax.random.uniform(jax.random.fold_in(jax.random.fold_in(key, 6), position), (parts,), jnp.float32, low / len(cuts), top_value / len(cuts))
        return jnp.repeat(jnp.exp(steps), dims[position] // parts).reshape((-1,) + (1,) * (len(dims) - position - 1))

    factor_of = one(*cuts[0])
    for cut in cuts[1:]:
        factor_of = factor_of * one(*cut)
    return factor_of


def assign_block(own_key, own, number, rows, amount, top, most, slope):
    order = jax.random.permutation(own_key, amount)
    heavy_load, usual = portions_of(amount, rows * top, most, slope, True), portions_of(amount, rows * top, most, slope, False)
    places = jnp.arange(amount)

    def named(sizes, offset_by):
        used = int((sizes > 0).sum())
        fixed = max(1, used // 4)
        moved = fixed + (places - fixed + offset_by * (used - fixed)) % max(1, amount - fixed)
        return jnp.zeros((amount,), jnp.int32).at[order[jnp.where(places < fixed, places, moved)]].set(jnp.asarray(sizes, jnp.int32))

    sizes = jnp.where(number % 4 == 0, named(heavy_load, number // 4), named(usual, number - number // 4 - 1))
    mixed = jax.random.permutation(jax.random.fold_in(own, 3), amount)
    source_of, sink = mixed[0:amount // 2 * 2:2], mixed[1:amount // 2 * 2:2]
    margin = jnp.minimum(sizes[source_of] - 1, most - sizes[sink]) // 2
    margin = jnp.where((source_of == order[0]) | (sink == order[0]) | (sizes[sink] == 0), 0, jnp.maximum(margin, 0))
    moved = jax.random.randint(jax.random.fold_in(own, 4), (amount // 2,), 0, 1 << 20) % (margin + 1)
    sizes = sizes.at[source_of].add(-moved).at[sink].add(moved)
    items = jnp.searchsorted(jnp.cumsum(sizes), jnp.arange(rows * top), side="right").astype(jnp.int32)
    table = items.reshape(top, rows).T
    table = table[jax.random.permutation(jax.random.fold_in(own, 1), rows)]
    offset_by = jax.random.randint(jax.random.fold_in(own, 2), (rows, 1), 0, top)
    return jnp.take_along_axis(table, (jnp.arange(top)[None, :] + offset_by) % top, axis=1)


def portions_of(amount, total, limit, slope, full):
    weights = [(1 << 20) // math.isqrt(grade ** slope) + 1 for grade in range(1, amount + 1)]
    largest = limit if full else min(limit, max(-(-total // amount), total * weights[0] // sum(weights)))
    least = 1 if total - largest >= amount - 1 else 0
    given, rest = [largest] + [least] * (amount - 1), total - largest - least * (amount - 1)
    while rest > 0:
        movable = [i for i in range(1, amount) if given[i] < largest] or [i for i in range(1, amount) if given[i] < limit]
        mass, budget = sum([weights[i] for i in movable]), rest
        for i in movable:
            extra = min(limit - given[i], max(1, budget * weights[i] // mass), rest)
            given[i] = given[i] + extra
            rest = rest - extra
    return np.array(given)


def bell_draw(rng, dims, spread, bound, split=(), held_as=jnp.bfloat16):
    values = jax.random.normal(rng, dims, jnp.float32) * spread
    if len(split) > 0:
        values = level_of(rng, dims, split, -0.22, 0.18) * values
    return jnp.clip(values, min=-bound, max=bound).astype(held_as)


def setup_inputs(seed: int = 0) -> dict:
    splits = jax.random.split(jax.random.key(seed), 4)
    jacobian = bell_draw(splits[0], (NPOINTS, 3, 3, F), (12 * PT) ** -0.5, 0.15625, ((0, 512),))
    owner_keys = jax.random.split(jax.random.fold_in(splits[1], 1), NPOINTS // PT)
    owner_turns = jax.random.permutation(jax.random.fold_in(splits[1], 3), NPOINTS // PT)
    owner = jax.vmap(lambda own, number: assign_block(jax.random.fold_in(splits[1], 2), own, number, PT, N_PTS, 1, CAP, 2))(owner_keys, owner_turns).reshape((NPOINTS, 1))
    damping = jnp.clip(jnp.exp(math.log(2.0) - 2.3025851 * jax.random.uniform(splits[2], (NE, F), jnp.float32) ** level_of(splits[2], (NE, F), ((0, 128),), -0.2, 0.2)), 0.2, 2.0)
    return {"jacobian": jacobian, "owner": owner, "damping": damping}


def gram(left, right):
    return lax.dot_general(left.astype(jnp.float32), right.astype(jnp.float32), (((0,), (0,)), ((), ())), preferred_element_type=jnp.float32)

def exact_gram(left, right):
    return lax.dot_general(left.astype(jnp.float32), right.astype(jnp.float32), (((0,), (0,)), ((), ())), precision=lax.Precision.HIGHEST, preferred_element_type=jnp.float32)

def reference(jacobian, owner, damping):
    window = N_PTS * N_GRP * CAP
    width = jacobian.shape[3]
    segment = owner[:, 0].astype(jnp.int32)
    order = jnp.argsort(segment, stable=True)
    sorted_rows = jacobian[order]
    counts = jax.ops.segment_sum(jnp.ones_like(segment), segment, num_segments=NE).astype(jnp.int32)
    starts = (jnp.cumsum(counts) - counts).astype(jnp.int32)
    padded = jnp.concatenate([sorted_rows, jnp.zeros((window, 3, 3, width), jacobian.dtype)], 0)

    def one_segment(items):
        start, count, lm_row = items
        rows = lax.dynamic_slice_in_dim(padded, start.astype(jnp.int32), window, 0)
        keep = jnp.arange(window, dtype=jnp.int32) < count
        rows = jnp.where(keep[:, None, None, None], rows, jnp.zeros_like(rows))
        first = rows[:, 0].reshape(window * 3, width)
        middle = rows[:, 1].reshape(window * 3, width)
        last = rows[:, 2].reshape(window * 3, width)
        d_low = gram(first, first)
        d_odd = gram(middle, middle)
        d_high = gram(last, last)
        b_low = gram(middle, first)
        b_high = gram(middle, last)
        e_pair = gram(first, last)
        system = d_odd + jnp.diag(lm_row)
        factor = jnp.linalg.cholesky(system)
        y_low = lax.linalg.triangular_solve(factor, b_low, left_side=True, lower=True)
        y_high = lax.linalg.triangular_solve(factor, b_high, left_side=True, lower=True)
        low = d_low - exact_gram(y_low, y_low)
        high = d_high - exact_gram(y_high, y_high)
        pair = e_pair - exact_gram(y_low, y_high)
        return (low, high, pair)
    low, high, pair = lax.map(one_segment, (starts, counts, damping))
    reduced_diag = low + jnp.roll(high, 1, axis=0)
    return (reduced_diag, pair)
```

```python
import jax
import jax.numpy as jnp
from jax import lax
from jax.experimental import pallas as pl
from jax.experimental.pallas import tpu as pltpu
from jax.sharding import Mesh
from jax.sharding import PartitionSpec as P

PTS = ("pts_0", "pts_1", "pts_2")
PTS_GRP = ("pts_0", "pts_1", "pts_2", "grp")
F32 = jnp.float32
BF16 = jnp.bfloat16
HI = lax.Precision.HIGHEST
NN = ((1,), (0,))
NT = ((1,), (1,))
TN = ((0,), (0,))
TILE = 128
PARAMS = pltpu.CompilerParams(vmem_limit_bytes=40 * 2**20)


def mm(a, b, dims, prec=None):
    return lax.dot_general(a, b, (dims, ((), ())), precision=prec, preferred_element_type=F32)


def call(body, outs, *args, cost=None, scratch=()):
    return pl.pallas_call(
        body, out_shape=outs, scratch_shapes=scratch, compiler_params=PARAMS, cost_estimate=cost
    )(*args)


def cost(flops, nbytes):
    return pl.CostEstimate(flops=flops, bytes_accessed=nbytes, transcendentals=0)


def pack_body(capacity, owner_ref, rows_ref, out_ref):
    clusters, sets, points, width = rows_ref.shape
    slots = out_ref.shape[0] * capacity
    owner = owner_ref[...]
    slot = lax.broadcasted_iota(jnp.int32, (slots, points), 0)
    hit = jnp.where(owner == slot // capacity, 1.0, 0.0)
    upper = jnp.where(
        lax.broadcasted_iota(jnp.int32, (points, points), 0)
        < lax.broadcasted_iota(jnp.int32, (points, points), 1),
        1.0,
        0.0,
    )
    before = mm(hit.astype(BF16), upper.astype(BF16), NN)
    pick = jnp.where(before == (slot % capacity).astype(F32), hit, 0.0).astype(BF16)
    for k in range(clusters):
        for r in range(sets):
            at = (k * sets + r) * width
            rows = mm(pick, rows_ref[k, r], NN).astype(BF16)
            out_ref[:, :, at : at + width] = rows.reshape(-1, capacity, width)


def cluster_rows(ref, k):
    width = ref.shape[2] // 9
    at = k * 3 * width
    flat = ref[:, :, at : at + 3 * width].reshape(-1, 3 * width)
    return [flat[:, r * width : (r + 1) * width] for r in range(3)]


def summed_gram(left, right):
    return mm(left[0], right[0], TN) + mm(left[1], right[1], TN) + mm(left[2], right[2], TN)


def odd_body(rows_ref, out_ref):
    mid = cluster_rows(rows_ref, 1)
    full = summed_gram(mid, mid)
    at = 0
    for i in range(full.shape[0] // TILE):
        for j in range(i + 1):
            out_ref[at : at + TILE] = full[i * TILE : (i + 1) * TILE, j * TILE : (j + 1) * TILE]
            at += TILE


def side_body(rows_ref, out_ref):
    width = out_ref.shape[0]
    mid = cluster_rows(rows_ref, 1)
    out_ref[:, :width] = summed_gram(cluster_rows(rows_ref, 0), mid)
    out_ref[:, width:] = summed_gram(cluster_rows(rows_ref, 2), mid)


def even_body(rows_ref, out_ref):
    width = out_ref.shape[0]
    first, last = cluster_rows(rows_ref, 0), cluster_rows(rows_ref, 2)
    out_ref[:, :width] = summed_gram(first, first)
    out_ref[:, width : 2 * width] = summed_gram(last, last)
    out_ref[:, 2 * width :] = summed_gram(last, first)


def sum_body(parts_ref, out_ref):
    total = parts_ref[0]
    for k in range(1, parts_ref.shape[0]):
        total = total + parts_ref[k]
    for k in range(out_ref.shape[0]):
        out_ref[k] = total


def eye(n):
    rows = lax.broadcasted_iota(jnp.int32, (n, n), 0)
    return jnp.where(rows == lax.broadcasted_iota(jnp.int32, (n, n), 1), 1.0, 0.0).astype(F32)


def factor_tile(a_ref, w_ref, panel):
    n = a_ref.shape[0]
    row = lax.broadcasted_iota(jnp.int32, (panel, n), 0)
    for b in range(0, n, panel):
        pa = a_ref[b : b + panel, :]
        pw = w_ref[b : b + panel, :]
        cols = [jnp.broadcast_to(pa[:, b + k : b + k + 1], (panel, n)) for k in range(panel)]
        scale = jnp.ones((panel, n), F32)
        for j in range(panel):
            pivot = jnp.broadcast_to(cols[j][j : j + 1, :], (panel, n))
            scale = jnp.where(row == j, pivot, scale)
            m = jnp.where(row > j, cols[j] / pivot, 0.0)
            for k in range(j + 1, panel):
                cols[k] = cols[k] - m * cols[k][j : j + 1, :]
            pa = pa - m * pa[j : j + 1, :]
            pw = pw - m * pw[j : j + 1, :]
        rs = lax.rsqrt(scale)
        pa = pa * rs
        pw = pw * rs
        w_ref[b : b + panel, :] = pw
        if b + panel < n:
            u = mm(pa, jnp.concatenate([pa, pw], axis=1), TN, HI)
            a_ref[b + panel :, :] = a_ref[b + panel :, :] - u[b + panel :, :n]
            w_ref[b + panel :, :] = w_ref[b + panel :, :] - u[b + panel :, n:]


def factor_body(blocks_ref, damping_ref, out_ref, a_ref, w_ref):
    n = TILE
    count = damping_ref.shape[1] // n
    at, s = 0, []
    for i in range(count):
        s.append([])
        for j in range(i + 1):
            s[i].append(blocks_ref[at : at + n])
            at += n
    for i in range(count):
        s[i][i] = s[i][i] + eye(n) * damping_ref[:, i * n : (i + 1) * n]
    for d in range(count):
        a_ref[...] = s[d][d]
        w_ref[...] = eye(n)
        factor_tile(a_ref, w_ref, 32)
        w = w_ref[...]
        out_ref[(d * (d + 1) // 2 + d) * n : (d * (d + 1) // 2 + d + 1) * n] = w
        for i in range(d + 1, count):
            s[i][d] = mm(s[i][d], w, NT, HI)
            out_ref[(i * (i + 1) // 2 + d) * n : (i * (i + 1) // 2 + d + 1) * n] = s[i][d]
        for i in range(d + 1, count):
            for k in range(d + 1, i + 1):
                s[i][k] = s[i][k] - mm(s[i][d], s[k][d], NT, HI)


def solve_body(factor_ref, right_ref, low_ref, high_ref):
    n = TILE
    rows, width = right_ref.shape[1], right_ref.shape[2] // 2
    count = width // n
    block = lambda i, j: factor_ref[(i * (i + 1) // 2 + j) * n : (i * (i + 1) // 2 + j + 1) * n]
    right = right_ref[0]
    for k in range(1, right_ref.shape[0]):
        right = right + right_ref[k]
    right = jnp.concatenate([right[:, :width], right[:, width:]], axis=0)
    done = []
    for i in range(count):
        part = right[:, i * n : (i + 1) * n]
        for j in range(i):
            part = part - mm(done[j], block(i, j), NT, HI)
        done.append(mm(part, block(i, i), NT, HI))
        for k in range(low_ref.shape[0]):
            low_ref[k, :, i * n : (i + 1) * n] = done[i][:rows]
            high_ref[k, :, i * n : (i + 1) * n] = done[i][rows:]


def whole(ref):
    return jnp.concatenate([ref[k] for k in range(ref.shape[0])], axis=0)


def high_body(y_ref, mine_ref, even_ref, out_ref):
    width = y_ref.shape[2]
    out_ref[...] = even_ref[:, width : 2 * width] - mm(mine_ref[0], whole(y_ref), NT, HI)


def low_body(y_ref, low_mine_ref, high_mine_ref, even_ref, low_ref, pair_ref):
    width = y_ref.shape[2]
    y_low = whole(y_ref)
    low_ref[...] = even_ref[:, :width] - mm(low_mine_ref[0], y_low, NT, HI)
    pair_ref[...] = even_ref[:, 2 * width :] - mm(high_mine_ref[0], y_low, NT, HI)


def exchanged(value, axis):
    return lax.all_to_all(value, axis, 0, 0, tiled=True)


def after(value, other):
    return lax.optimization_barrier((value, other))[0]


def shape(*dims):
    return jax.ShapeDtypeStruct(dims, F32)


def local(jacobian, owner, damping):
    points, _, _, width = jacobian.shape
    owners = lax.axis_size(PTS)
    groups = lax.axis_size("grp")
    columns = width // groups
    capacity = max(2, 2 * points // owners)
    rows = jnp.transpose(jacobian, (1, 2, 0, 3))
    segment = owner.reshape(1, points)
    tiles = (width // TILE) * (width // TILE + 1) // 2

    sent = call(
        lambda *refs: pack_body(capacity, *refs),
        jax.ShapeDtypeStruct((owners, capacity, 9 * width), BF16),
        segment,
        rows,
    )
    got = exchanged(sent, PTS)
    odd = call(odd_body, shape(tiles * TILE, TILE), got, cost=cost(10**9, 10**6))
    odd = exchanged(odd.reshape(groups, -1, TILE), "grp")
    odd = call(sum_body, shape(*odd.shape), odd)
    odd = exchanged(odd, "grp").reshape(-1, TILE)
    even = call(even_body, shape(width, 3 * width), got, cost=cost(10**9, 10**6))
    even = lax.psum_scatter(even, "grp", scatter_dimension=0, tiled=True)
    side = call(side_body, shape(width, 2 * width), got, cost=cost(10**9, 10**6))
    side = after(side, odd)
    side = exchanged(side.reshape(groups, columns, 2 * width), "grp")
    factor = call(
        factor_body,
        shape(tiles * TILE, TILE),
        odd,
        damping,
        cost=cost(10**10, 10**6),
        scratch=[pltpu.VMEM((TILE, TILE), F32)] * 2,
    )
    pieces = shape(groups, columns, width)
    low_mine, high_mine = call(solve_body, (pieces, pieces), factor, side)
    y_high = exchanged(high_mine, "grp")
    high = call(high_body, shape(columns, width), y_high, high_mine, even)
    carried = lax.ppermute(high, PTS, [(i, (i + 1) % owners) for i in range(owners)])
    y_low = exchanged(low_mine, "grp")
    low, pair = call(
        low_body,
        (shape(columns, width), shape(columns, width)),
        y_low,
        low_mine,
        high_mine,
        even,
    )
    return ((low + carried).T[None], pair.T[None])


def solution(mesh):
    torus = Mesh(
        mesh.devices.reshape(8, 8, 2, mesh.shape["grp"]), ("pts_0", "pts_1", "pts_2", "grp")
    )
    placed = (P(PTS_GRP, None, None, None), P(PTS_GRP, None), P(PTS, None))
    return jax.shard_map(
        local,
        mesh=torus,
        in_specs=placed,
        out_specs=(P(PTS, None, "grp"), P(PTS, None, "grp")),
        check_vma=False,
    )
```

```python
import jax
import jax.numpy as jnp
from jax import lax
from jax.experimental import pallas as pl
from jax.experimental.pallas import tpu as pltpu
from jax.sharding import Mesh
from jax.sharding import PartitionSpec as P

PTS = ("pts_0", "pts_1", "pts_2")
PTS_GRP = ("pts_0", "pts_1", "pts_2", "grp")
F32 = jnp.float32
BF16 = jnp.bfloat16
HI = lax.Precision.HIGHEST
NN = ((1,), (0,))
NT = ((1,), (1,))
TN = ((0,), (0,))
TILE = 128
SUB = 8
PARAMS = pltpu.CompilerParams(vmem_limit_bytes=40 * 2**20)


def mm(a, b, dims, prec=None):
    return lax.dot_general(a, b, (dims, ((), ())), precision=prec, preferred_element_type=F32)


def call(body, outs, *args, cost=None, scratch=(), scalars=0):
    places = [pltpu.SMEM] * scalars + [pltpu.VMEM] * (len(args) - scalars)
    return pl.pallas_call(
        body,
        out_shape=outs,
        in_specs=[pl.BlockSpec(memory_space=place) for place in places],
        scratch_shapes=scratch,
        compiler_params=PARAMS,
        cost_estimate=cost,
    )(*args)


def cost(flops, nbytes):
    return pl.CostEstimate(flops=flops, bytes_accessed=nbytes, transcendentals=0)


def pack_body(capacity, owner_ref, rows_ref, out_ref):
    clusters, sets, points, width = rows_ref.shape
    slots = out_ref.shape[0] * capacity
    owner = owner_ref[...]
    slot = lax.broadcasted_iota(jnp.int32, (slots, points), 0)
    hit = jnp.where(owner == slot // capacity, 1.0, 0.0)
    upper = jnp.where(
        lax.broadcasted_iota(jnp.int32, (points, points), 0)
        < lax.broadcasted_iota(jnp.int32, (points, points), 1),
        1.0,
        0.0,
    )
    before = mm(hit.astype(BF16), upper.astype(BF16), NN)
    pick = jnp.where(before == (slot % capacity).astype(F32), hit, 0.0).astype(BF16)
    for k in range(clusters):
        for r in range(sets):
            at = (k * sets + r) * width
            rows = mm(pick, rows_ref[k, r], NN).astype(BF16)
            out_ref[:, :, at : at + width] = rows.reshape(-1, capacity, width)


def cluster_rows(ref, k):
    width = ref.shape[2] // 9
    at = k * 3 * width
    flat = ref[:, :, at : at + 3 * width].reshape(-1, 3 * width)
    return [flat[:, r * width : (r + 1) * width] for r in range(3)]


def summed_gram(left, right):
    return mm(left[0], right[0], TN) + mm(left[1], right[1], TN) + mm(left[2], right[2], TN)


def odd_body(rows_ref, out_ref):
    mid = cluster_rows(rows_ref, 1)
    full = summed_gram(mid, mid)
    at = 0
    for i in range(full.shape[0] // TILE):
        for j in range(i + 1):
            block = full[i * TILE : (i + 1) * TILE, j * TILE : (j + 1) * TILE]
            for k in range(out_ref.shape[0]):
                out_ref[k, at : at + TILE] = block
            at += TILE


def side_body(index_ref, rows_ref, *refs):
    piece_refs, full_ref = refs[:-1], refs[-1]
    width = full_ref.shape[0]
    columns = piece_refs[0].shape[0]
    mid = cluster_rows(rows_ref, 1)
    full_ref[:, :width] = summed_gram(cluster_rows(rows_ref, 0), mid)
    full_ref[:, width:] = summed_gram(cluster_rows(rows_ref, 2), mid)
    for k, piece_ref in enumerate(piece_refs):
        at = lax.rem(index_ref[0] + k, len(piece_refs))
        piece_ref[...] = full_ref[pl.ds(pl.multiple_of(at * columns, 8), columns), :]


def even_body(rows_ref, out_ref, last_ref):
    width = last_ref.shape[0]
    first, last = cluster_rows(rows_ref, 0), cluster_rows(rows_ref, 2)
    last_ref[...] = summed_gram(last, last)
    out_ref[:, :width] = summed_gram(first, first)
    out_ref[:, width:] = summed_gram(last, first)


def join_body(even_ref, last_ref, out_ref):
    width = last_ref.shape[0]
    out_ref[:, :width] = even_ref[:, :width] + last_ref[...]
    out_ref[:, width:] = even_ref[:, width:]


def eye(n):
    rows = lax.broadcasted_iota(jnp.int32, (n, n), 0)
    return jnp.where(rows == lax.broadcasted_iota(jnp.int32, (n, n), 1), 1.0, 0.0).astype(F32)


def factor_tile(a_ref, w_ref, panel):
    n = a_ref.shape[0]
    tiles = panel // SUB
    row = lax.broadcasted_iota(jnp.int32, (SUB, n), 0)

    def splat(value, r):
        return jnp.broadcast_to(value[r : r + 1, :], (SUB, n))

    for b in range(0, n, panel):
        pa = [a_ref[b + t * SUB : b + (t + 1) * SUB, :] for t in range(tiles)]
        pw = [w_ref[b + t * SUB : b + (t + 1) * SUB, :] for t in range(tiles)]
        for top in range(tiles):
            at = b + top * SUB
            cols = [
                {t: jnp.broadcast_to(pa[t][:, at + k : at + k + 1], (SUB, n)) for t in range(top, tiles)}
                for k in range(SUB)
            ]
            scale = jnp.ones((SUB, n), F32)
            for r in range(0, SUB, 2):
                p = splat(cols[r][top], r)
                q = splat(cols[r][top], r + 1)
                c = splat(cols[r + 1][top], r + 1)
                over = 1.0 / (p * c - q * q)
                g0, g1, g2 = c * over, q * over, p * over
                h = q * (1.0 / p)
                scale = jnp.where(row == r, p, jnp.where(row == r + 1, c - q * h, scale))
                first = top if r + 2 < SUB else top + 1
                m0, m1 = {}, {}
                for t in range(first, tiles):
                    c0, c1 = cols[r][t], cols[r + 1][t]
                    m0[t] = c0 * g0 - c1 * g1
                    m1[t] = c1 * g2 - c0 * g1
                    if t == top:
                        m0[t] = jnp.where(row > r + 1, m0[t], 0.0)
                        m1[t] = jnp.where(row > r + 1, m1[t], 0.0)
                for k in range(r + 2, SUB):
                    s0, s1 = splat(cols[k][top], r), splat(cols[k][top], r + 1)
                    for t in range(first, tiles):
                        cols[k][t] = cols[k][t] - m0[t] * s0 - m1[t] * s1
                for x in (pa, pw):
                    s0, s1 = splat(x[top], r), splat(x[top], r + 1)
                    for t in range(first, tiles):
                        x[t] = x[t] - m0[t] * s0 - m1[t] * s1
                    x[top] = jnp.where(row == r + 1, x[top] - h * s0, x[top])
            rs = lax.rsqrt(scale)
            pa[top] = pa[top] * rs
            pw[top] = pw[top] * rs
        left = jnp.concatenate(pa, axis=0)
        right = jnp.concatenate(pw, axis=0)
        w_ref[b : b + panel, :] = right
        if b + panel < n:
            u = mm(left, jnp.concatenate([left, right], axis=1), TN, HI)
            a_ref[b + panel :, :] = a_ref[b + panel :, :] - u[b + panel :, :n]
            w_ref[b + panel :, :] = w_ref[b + panel :, :] - u[b + panel :, n:]


def summed(ref, at, rows):
    value = ref[0, at : at + rows]
    for k in range(1, ref.shape[0]):
        value = value + ref[k, at : at + rows]
    return value


def factor_body(blocks_ref, damping_ref, out_ref, a_ref, w_ref):
    n = TILE
    count = damping_ref.shape[1] // n
    at, s = 0, []
    for i in range(count):
        s.append([])
        for j in range(i + 1):
            s[i].append(summed(blocks_ref, at, n))
            at += n
    for i in range(count):
        s[i][i] = s[i][i] + eye(n) * damping_ref[:, i * n : (i + 1) * n]
    for d in range(count):
        a_ref[...] = s[d][d]
        w_ref[...] = eye(n)
        factor_tile(a_ref, w_ref, 64)
        w = w_ref[...]
        out_ref[(d * (d + 1) // 2 + d) * n : (d * (d + 1) // 2 + d + 1) * n] = w
        for i in range(d + 1, count):
            s[i][d] = mm(s[i][d], w, NT, HI)
            out_ref[(i * (i + 1) // 2 + d) * n : (i * (i + 1) // 2 + d + 1) * n] = s[i][d]
        for i in range(d + 1, count):
            for k in range(d + 1, i + 1):
                s[i][k] = s[i][k] - mm(s[i][d], s[k][d], NT, HI)


def solve_body(factor_ref, *refs):
    right_refs, (low_ref, high_ref) = refs[:-2], refs[-2:]
    n = TILE
    rows, width = right_refs[0].shape[0], right_refs[0].shape[1] // 2
    count = width // n
    block = lambda i, j: factor_ref[(i * (i + 1) // 2 + j) * n : (i * (i + 1) // 2 + j + 1) * n]
    right = right_refs[0][...]
    for ref in right_refs[1:]:
        right = right + ref[...]
    right = jnp.concatenate([right[:, :width], right[:, width:]], axis=0)
    done = []
    for i in range(count):
        part = right[:, i * n : (i + 1) * n]
        for j in range(i):
            part = part - mm(done[j], block(i, j), NT, HI)
        done.append(mm(part, block(i, i), NT, HI))
        for k in range(low_ref.shape[0]):
            low_ref[k, :, i * n : (i + 1) * n] = done[i][:rows]
            high_ref[k, :, i * n : (i + 1) * n] = done[i][rows:]


def whole(ref):
    return jnp.concatenate([ref[k] for k in range(ref.shape[0])], axis=0)


def total_body(parts_ref, out_ref):
    value = parts_ref[0]
    for k in range(1, parts_ref.shape[0]):
        value = value + parts_ref[k]
    out_ref[...] = value


def high_body(y_ref, mine_ref, out_ref):
    out_ref[...] = mm(mine_ref[0], whole(y_ref), NT, HI)


def low_body(y_ref, low_mine_ref, high_mine_ref, even_ref, high_ref, diag_ref, pair_ref):
    columns, width = high_ref.shape
    mine = jnp.concatenate([low_mine_ref[0], high_mine_ref[0]], axis=0)
    u = mm(mine, whole(y_ref), NT, HI)
    diag_ref[...] = even_ref[:, :width] - u[:columns] - high_ref[...]
    pair_ref[...] = even_ref[:, width:] - u[columns:]


def exchanged(value, axis):
    return lax.all_to_all(value, axis, 0, 0, tiled=True)


def turned(value, axis, by):
    if by == 0:
        return value
    devices = lax.axis_size(axis)
    return lax.ppermute(value, axis, [(i, (i + by) % devices) for i in range(devices)])


def after(value, other):
    return lax.optimization_barrier((value, other))[0]


def shape(*dims):
    return jax.ShapeDtypeStruct(dims, F32)


def local(jacobian, owner, damping):
    points, _, _, width = jacobian.shape
    owners = lax.axis_size(PTS)
    groups = lax.axis_size("grp")
    columns = width // groups
    capacity = max(2, 2 * points // owners)
    rows = jnp.transpose(jacobian, (1, 2, 0, 3))
    segment = owner.reshape(1, points)
    tiles = (width // TILE) * (width // TILE + 1) // 2

    sent = call(
        lambda *refs: pack_body(capacity, *refs),
        jax.ShapeDtypeStruct((owners, capacity, 9 * width), BF16),
        segment,
        rows,
    )
    got = exchanged(sent, PTS)
    odd = call(odd_body, shape(groups, tiles * TILE, TILE), got, cost=cost(10**9, 10**6))
    odd = exchanged(odd, "grp")
    even, last = call(
        even_body, [shape(width, 2 * width), shape(width, width)], got, cost=cost(10**9, 10**6)
    )
    carried = turned(last, PTS, 1)
    index = lax.axis_index("grp").astype(jnp.int32).reshape(1)
    side = call(
        side_body,
        [shape(columns, 2 * width)] * groups,
        index,
        got,
        cost=cost(10**9, 10**6),
        scratch=[pltpu.VMEM((width, 2 * width), F32)],
        scalars=1,
    )
    side = [turned(piece, "grp", k) for k, piece in enumerate(side)]
    even = call(join_body, shape(width, 2 * width), even, carried)
    even = exchanged(after(even, odd).reshape(groups, columns, 2 * width), "grp")
    factor = call(
        factor_body,
        shape(tiles * TILE, TILE),
        odd,
        damping,
        cost=cost(10**10, 10**6),
        scratch=[pltpu.VMEM((TILE, TILE), F32)] * 2,
    )
    low_mine, high_mine = call(
        solve_body, [shape(groups, columns, width)] * 2, factor, *side
    )
    high_mine, even = lax.optimization_barrier((high_mine, even))
    y_high = exchanged(high_mine, "grp")
    even = call(total_body, shape(columns, 2 * width), even)
    high = call(high_body, shape(columns, width), y_high, high_mine)
    high = turned(high, PTS, 1)
    low_mine, y_high = lax.optimization_barrier((low_mine, y_high))
    y_low = exchanged(low_mine, "grp")
    diag, pair = call(
        low_body, [shape(columns, width)] * 2, y_low, low_mine, high_mine, even, high
    )
    return (diag.T[None], pair.T[None])


def solution(mesh):
    torus = Mesh(
        mesh.devices.reshape(8, 8, 2, mesh.shape["grp"]), ("pts_0", "pts_1", "pts_2", "grp")
    )
    placed = (P(PTS_GRP, None, None, None), P(PTS_GRP, None), P(PTS, None))
    return jax.shard_map(
        local,
        mesh=torus,
        in_specs=placed,
        out_specs=(P(PTS, None, "grp"), P(PTS, None, "grp")),
        check_vma=False,
    )
```

```python
import jax
import jax.numpy as jnp
from jax import lax
from jax.experimental import pallas as pl
from jax.experimental.pallas import tpu as pltpu
from jax.sharding import Mesh
from jax.sharding import PartitionSpec as P

PTS = ("pts_0", "pts_1", "pts_2")
PTS_GRP = ("pts_0", "pts_1", "pts_2", "grp")
F32 = jnp.float32
BF16 = jnp.bfloat16
HI = lax.Precision.HIGHEST
NN = ((1,), (0,))
NT = ((1,), (1,))
TN = ((0,), (0,))
TILE = 128
SUB = 8
PARAMS = pltpu.CompilerParams(vmem_limit_bytes=40 * 2**20)


def mm(a, b, dims, prec=None):
    return lax.dot_general(a, b, (dims, ((), ())), precision=prec, preferred_element_type=F32)


def call(body, outs, *args, cost=None, scratch=(), scalars=0):
    places = [pltpu.SMEM] * scalars + [pltpu.VMEM] * (len(args) - scalars)
    return pl.pallas_call(
        body,
        out_shape=outs,
        in_specs=[pl.BlockSpec(memory_space=place) for place in places],
        scratch_shapes=scratch,
        compiler_params=PARAMS,
        cost_estimate=cost,
    )(*args)


def cost(flops, nbytes):
    return pl.CostEstimate(flops=flops, bytes_accessed=nbytes, transcendentals=0)


def pack_body(capacity, owner_ref, rows_ref, out_ref):
    clusters, sets, points, width = rows_ref.shape
    slots = out_ref.shape[0] * capacity
    owner = owner_ref[...]
    slot = lax.broadcasted_iota(jnp.int32, (slots, points), 0)
    hit = jnp.where(owner == slot // capacity, 1.0, 0.0)
    upper = jnp.where(
        lax.broadcasted_iota(jnp.int32, (points, points), 0)
        < lax.broadcasted_iota(jnp.int32, (points, points), 1),
        1.0,
        0.0,
    )
    before = mm(hit.astype(BF16), upper.astype(BF16), NN)
    pick = jnp.where(before == (slot % capacity).astype(F32), hit, 0.0).astype(BF16)
    for k in range(clusters):
        for r in range(sets):
            at = (k * sets + r) * width
            rows = mm(pick, rows_ref[k, r], NN).astype(BF16)
            out_ref[:, :, at : at + width] = rows.reshape(-1, capacity, width)


def cluster_rows(ref, k):
    width = ref.shape[2] // 9
    at = k * 3 * width
    flat = ref[:, :, at : at + 3 * width].reshape(-1, 3 * width)
    return [flat[:, r * width : (r + 1) * width] for r in range(3)]


def summed_gram(left, right):
    return mm(left[0], right[0], TN) + mm(left[1], right[1], TN) + mm(left[2], right[2], TN)


def odd_body(rows_ref, out_ref, packed_ref, sems):
    mid = cluster_rows(rows_ref, 1)
    full = summed_gram(mid, mid)
    count = full.shape[0] // TILE
    block = lambda i, j: full[i * TILE : (i + 1) * TILE, j * TILE : (j + 1) * TILE]
    lower = lax.broadcasted_iota(jnp.int32, (TILE, TILE), 0) >= lax.broadcasted_iota(
        jnp.int32, (TILE, TILE), 1
    )
    packed_ref[:TILE] = jnp.where(lower, block(0, 0), block(1, 1))
    at = TILE
    for i in range(1, count):
        for j in range(i + 1):
            if (i, j) != (1, 1):
                packed_ref[at : at + TILE] = block(i, j)
                at += TILE
    diagonal = jnp.sum(block(1, 1) * eye(TILE), axis=0, keepdims=True)
    packed_ref[at:] = jnp.broadcast_to(diagonal, (SUB, TILE))
    copies = [
        pltpu.make_async_copy(packed_ref, out_ref.at[k], sems.at[k])
        for k in range(out_ref.shape[0])
    ]
    for copy in copies:
        copy.start()
    for copy in copies:
        copy.wait()


def side_body(index_ref, rows_ref, *refs):
    piece_refs, full_ref = refs[:-1], refs[-1]
    width = full_ref.shape[0]
    columns = piece_refs[0].shape[0]
    mid = cluster_rows(rows_ref, 1)
    full_ref[:, :width] = summed_gram(cluster_rows(rows_ref, 0), mid)
    full_ref[:, width:] = summed_gram(cluster_rows(rows_ref, 2), mid)
    for k, piece_ref in enumerate(piece_refs):
        at = lax.rem(index_ref[0] + k, len(piece_refs))
        piece_ref[...] = full_ref[pl.ds(pl.multiple_of(at * columns, 8), columns), :]


def last_body(rows_ref, out_ref):
    last = cluster_rows(rows_ref, 2)
    out_ref[...] = summed_gram(last, last)


def even_body(rows_ref, carried_ref, out_ref):
    width = carried_ref.shape[0]
    first, last = cluster_rows(rows_ref, 0), cluster_rows(rows_ref, 2)
    out_ref[:, :width] = summed_gram(first, first) + carried_ref[...]
    out_ref[:, width:] = summed_gram(last, first)


def eye(n):
    rows = lax.broadcasted_iota(jnp.int32, (n, n), 0)
    return jnp.where(rows == lax.broadcasted_iota(jnp.int32, (n, n), 1), 1.0, 0.0).astype(F32)


def factor_tile(a_ref, w_ref, panel):
    n = a_ref.shape[0]
    tiles = panel // SUB
    row = lax.broadcasted_iota(jnp.int32, (SUB, n), 0)

    def splat(value, r):
        return jnp.broadcast_to(value[r : r + 1, :], (SUB, n))

    for b in range(0, n, panel):
        pa = [a_ref[b + t * SUB : b + (t + 1) * SUB, :] for t in range(tiles)]
        pw = [w_ref[b + t * SUB : b + (t + 1) * SUB, :] for t in range(tiles)]
        for top in range(tiles):
            at = b + top * SUB
            cols = [
                {t: jnp.broadcast_to(pa[t][:, at + k : at + k + 1], (SUB, n)) for t in range(top, tiles)}
                for k in range(SUB)
            ]
            scale = jnp.ones((SUB, n), F32)
            for r in range(0, SUB, 2):
                p = splat(cols[r][top], r)
                q = splat(cols[r][top], r + 1)
                c = splat(cols[r + 1][top], r + 1)
                over = 1.0 / (p * c - q * q)
                g0, g1, g2 = c * over, q * over, p * over
                h = q * (1.0 / p)
                scale = jnp.where(row == r, p, jnp.where(row == r + 1, c - q * h, scale))
                first = top if r + 2 < SUB else top + 1
                m0, m1 = {}, {}
                for t in range(first, tiles):
                    c0, c1 = cols[r][t], cols[r + 1][t]
                    m0[t] = c0 * g0 - c1 * g1
                    m1[t] = c1 * g2 - c0 * g1
                    if t == top:
                        m0[t] = jnp.where(row > r + 1, m0[t], 0.0)
                        m1[t] = jnp.where(row > r + 1, m1[t], 0.0)
                for k in range(r + 2, SUB):
                    s0, s1 = splat(cols[k][top], r), splat(cols[k][top], r + 1)
                    for t in range(first, tiles):
                        cols[k][t] = cols[k][t] - m0[t] * s0 - m1[t] * s1
                for x in (pa, pw):
                    s0, s1 = splat(x[top], r), splat(x[top], r + 1)
                    for t in range(first, tiles):
                        x[t] = x[t] - m0[t] * s0 - m1[t] * s1
                    x[top] = jnp.where(row == r + 1, x[top] - h * s0, x[top])
            rs = lax.rsqrt(scale)
            pa[top] = pa[top] * rs
            pw[top] = pw[top] * rs
        left = jnp.concatenate(pa, axis=0)
        right = jnp.concatenate(pw, axis=0)
        w_ref[b : b + panel, :] = right
        if b + panel < n:
            u = mm(left, jnp.concatenate([left, right], axis=1), TN, HI)
            a_ref[b + panel :, :] = a_ref[b + panel :, :] - u[b + panel :, :n]
            w_ref[b + panel :, :] = w_ref[b + panel :, :] - u[b + panel :, n:]


def summed(ref, at, rows):
    value = ref[0, at : at + rows]
    for k in range(1, ref.shape[0]):
        value = value + ref[k, at : at + rows]
    return value


def factor_body(blocks_ref, damping_ref, out_ref, a_ref, w_ref):
    n = TILE
    count = damping_ref.shape[1] // n
    packed = summed(blocks_ref, 0, n)
    turned_over = packed.T
    row = lax.broadcasted_iota(jnp.int32, (n, n), 0)
    col = lax.broadcasted_iota(jnp.int32, (n, n), 1)
    at, s = n, [[jnp.where(row >= col, packed, turned_over)]]
    for i in range(1, count):
        s.append([])
        for j in range(i + 1):
            if (i, j) != (1, 1):
                s[i].append(summed(blocks_ref, at, n))
                at += n
            else:
                s[i].append(jnp.where(row < col, packed, turned_over))
    diagonal = summed(blocks_ref, at, SUB)[:1]
    s[1][1] = jnp.where(row == col, diagonal, s[1][1])
    for i in range(count):
        s[i][i] = s[i][i] + eye(n) * damping_ref[:, i * n : (i + 1) * n]
    for d in range(count - 1):
        a_ref[...] = s[d][d]
        w_ref[...] = eye(n)
        factor_tile(a_ref, w_ref, 64)
        w = w_ref[...]
        out_ref[(d * (d + 1) // 2 + d) * n : (d * (d + 1) // 2 + d + 1) * n] = w
        for i in range(d + 1, count):
            s[i][d] = mm(s[i][d], w, NT, HI)
            out_ref[(i * (i + 1) // 2 + d) * n : (i * (i + 1) // 2 + d + 1) * n] = s[i][d]
        for i in range(d + 1, count):
            for k in range(d + 1, i + 1):
                s[i][k] = s[i][k] - mm(s[i][d], s[k][d], NT, HI)
    out_ref[-n:] = s[-1][-1]


def solve_body(factor_ref, *refs):
    right_refs, (low_ref, high_ref, a_ref, w_ref) = refs[:-4], refs[-4:]
    n = TILE
    rows, width = right_refs[0].shape[0], right_refs[0].shape[1] // 2
    count = width // n
    block = lambda i, j: factor_ref[(i * (i + 1) // 2 + j) * n : (i * (i + 1) // 2 + j + 1) * n]
    a_ref[...] = block(count - 1, count - 1)
    w_ref[...] = eye(n)
    right = right_refs[0][...]
    for ref in right_refs[1:]:
        right = right + ref[...]
    right = jnp.concatenate([right[:, :width], right[:, width:]], axis=0)
    done = []
    for i in range(count):
        part = right[:, i * n : (i + 1) * n]
        for j in range(i):
            part = part - mm(done[j], block(i, j), NT, HI)
        if i == count - 1:
            factor_tile(a_ref, w_ref, 64)
            inverse = w_ref[...]
        else:
            inverse = block(i, i)
        done.append(mm(part, inverse, NT, HI))
        for k in range(low_ref.shape[0]):
            low_ref[k, :, i * n : (i + 1) * n] = done[i][:rows]
        high_ref[:, i * n : (i + 1) * n] = done[i][rows:]


def whole(ref):
    return jnp.concatenate([ref[k] for k in range(ref.shape[0])], axis=0)


def total_body(parts_ref, out_ref):
    value = parts_ref[0]
    for k in range(1, parts_ref.shape[0]):
        value = value + parts_ref[k]
    out_ref[...] = value


def high_body(y_ref, mine_ref, out_ref):
    out_ref[...] = mm(mine_ref[...], whole(y_ref), NT, HI)


def low_body(y_ref, low_mine_ref, high_mine_ref, even_ref, high_ref, diag_ref, pair_ref):
    columns, width = high_ref.shape
    mine = jnp.concatenate([low_mine_ref[0], high_mine_ref[...]], axis=0)
    u = mm(mine, whole(y_ref), NT, HI)
    diag_ref[...] = even_ref[:, :width] - u[:columns] - high_ref[...]
    pair_ref[...] = even_ref[:, width:] - u[columns:]


def exchanged(value, axis):
    return lax.all_to_all(value, axis, 0, 0, tiled=True)


def turned(value, axis, by):
    if by == 0:
        return value
    devices = lax.axis_size(axis)
    return lax.ppermute(value, axis, [(i, (i + by) % devices) for i in range(devices)])


def after(value, other):
    return lax.optimization_barrier((value, other))[0]


def shape(*dims):
    return jax.ShapeDtypeStruct(dims, F32)


def local(jacobian, owner, damping):
    points, _, _, width = jacobian.shape
    owners = lax.axis_size(PTS)
    groups = lax.axis_size("grp")
    columns = width // groups
    capacity = max(2, 2 * points // owners)
    rows = jnp.transpose(jacobian, (1, 2, 0, 3))
    segment = owner.reshape(1, points)
    tiles = (width // TILE) * (width // TILE + 1) // 2

    sent = call(
        lambda *refs: pack_body(capacity, *refs),
        jax.ShapeDtypeStruct((owners, capacity, 9 * width), BF16),
        segment,
        rows,
    )
    got = exchanged(sent, PTS)
    packed = (tiles - 1) * TILE + SUB
    odd = pl.pallas_call(
        odd_body,
        out_shape=shape(groups, packed, TILE),
        in_specs=[pl.BlockSpec(memory_space=pltpu.VMEM)],
        out_specs=pl.BlockSpec(memory_space=pltpu.HBM),
        scratch_shapes=[pltpu.VMEM((packed, TILE), F32), pltpu.SemaphoreType.DMA((groups,))],
        compiler_params=PARAMS,
        cost_estimate=cost(10**9, 10**6),
    )(got)
    odd = exchanged(odd, "grp")
    last = call(last_body, shape(width, width), got, cost=cost(10**9, 10**6))
    carried = turned(last, PTS, 1)
    index = lax.axis_index("grp").astype(jnp.int32).reshape(1)
    side = call(
        side_body,
        [shape(columns, 2 * width)] * groups,
        index,
        got,
        cost=cost(10**9, 10**6),
        scratch=[pltpu.VMEM((width, 2 * width), F32)],
        scalars=1,
    )
    side = [turned(piece, "grp", k) for k, piece in enumerate(side)]
    even = call(even_body, shape(width, 2 * width), got, carried, cost=cost(10**9, 10**6))
    even = exchanged(after(even, odd).reshape(groups, columns, 2 * width), "grp")
    factor = call(
        factor_body,
        shape(tiles * TILE, TILE),
        odd,
        damping,
        cost=cost(10**10, 10**6),
        scratch=[pltpu.VMEM((TILE, TILE), F32)] * 2,
    )
    low_mine, high_mine = call(
        solve_body,
        [shape(groups, columns, width), shape(columns, width)],
        factor,
        *side,
        cost=cost(3 * 10**9, 10**6),
        scratch=[pltpu.VMEM((TILE, TILE), F32)] * 2,
    )
    y_high = lax.all_gather(high_mine, "grp", axis=0, tiled=False)
    low_mine, y_high, even = lax.optimization_barrier((low_mine, y_high, even))
    y_low = exchanged(low_mine, "grp")
    even = call(total_body, shape(columns, 2 * width), even)
    high = call(high_body, shape(columns, width), y_high, high_mine)
    high = turned(high, PTS, 1)
    diag, pair = call(
        low_body, [shape(columns, width)] * 2, y_low, low_mine, high_mine, even, high
    )
    return (diag.T[None], pair.T[None])


def solution(mesh):
    torus = Mesh(
        mesh.devices.reshape(8, 8, 2, mesh.shape["grp"]), ("pts_0", "pts_1", "pts_2", "grp")
    )
    placed = (P(PTS_GRP, None, None, None), P(PTS_GRP, None), P(PTS, None))
    return jax.shard_map(
        local,
        mesh=torus,
        in_specs=placed,
        out_specs=(P(PTS, None, "grp"), P(PTS, None, "grp")),
        check_vma=False,
    )
```

```python
import jax
import jax.numpy as jnp
from jax import lax
from jax.experimental import pallas as pl
from jax.experimental.pallas import tpu as pltpu
from jax.sharding import Mesh
from jax.sharding import PartitionSpec as P

PTS = ("pts_0", "pts_1", "pts_2")
PTS_GRP = ("pts_0", "pts_1", "pts_2", "grp")
F32 = jnp.float32
BF16 = jnp.bfloat16
HI = lax.Precision.HIGHEST
NN = ((1,), (0,))
NT = ((1,), (1,))
TN = ((0,), (0,))
TILE = 128
SUB = 8
PARAMS = pltpu.CompilerParams(vmem_limit_bytes=40 * 2**20)


def mm(a, b, dims, prec=None):
    return lax.dot_general(a, b, (dims, ((), ())), precision=prec, preferred_element_type=F32)


def call(body, outs, *args, cost=None, scratch=(), scalars=0):
    places = [pltpu.SMEM] * scalars + [pltpu.VMEM] * (len(args) - scalars)
    return pl.pallas_call(
        body,
        out_shape=outs,
        in_specs=[pl.BlockSpec(memory_space=place) for place in places],
        scratch_shapes=scratch,
        compiler_params=PARAMS,
        cost_estimate=cost,
    )(*args)


def cost(flops, nbytes):
    return pl.CostEstimate(flops=flops, bytes_accessed=nbytes, transcendentals=0)


def pack_body(capacity, owner_ref, rows_ref, out_ref):
    clusters, sets, points, width = rows_ref.shape
    slots = out_ref.shape[0] * capacity
    owner = owner_ref[...]
    slot = lax.broadcasted_iota(jnp.int32, (slots, points), 0)
    hit = jnp.where(owner == slot // capacity, 1.0, 0.0)
    upper = jnp.where(
        lax.broadcasted_iota(jnp.int32, (points, points), 0)
        < lax.broadcasted_iota(jnp.int32, (points, points), 1),
        1.0,
        0.0,
    )
    before = mm(hit.astype(BF16), upper.astype(BF16), NN)
    pick = jnp.where(before == (slot % capacity).astype(F32), hit, 0.0).astype(BF16)
    for k in range(clusters):
        for r in range(sets):
            at = (k * sets + r) * width
            rows = mm(pick, rows_ref[k, r], NN).astype(BF16)
            out_ref[:, :, at : at + width] = rows.reshape(-1, capacity, width)


def cluster_rows(ref, k):
    width = ref.shape[2] // 9
    at = k * 3 * width
    flat = ref[:, :, at : at + 3 * width].reshape(-1, 3 * width)
    return [flat[:, r * width : (r + 1) * width] for r in range(3)]


def summed_gram(left, right):
    return mm(left[0], right[0], TN) + mm(left[1], right[1], TN) + mm(left[2], right[2], TN)


def odd_body(rows_ref, out_ref, packed_ref, sems):
    mid = cluster_rows(rows_ref, 1)
    full = summed_gram(mid, mid)
    count = full.shape[0] // TILE
    block = lambda i, j: full[i * TILE : (i + 1) * TILE, j * TILE : (j + 1) * TILE]
    lower = lax.broadcasted_iota(jnp.int32, (TILE, TILE), 0) >= lax.broadcasted_iota(
        jnp.int32, (TILE, TILE), 1
    )
    packed_ref[:TILE] = jnp.where(lower, block(0, 0), block(1, 1))
    at = TILE
    for i in range(1, count):
        for j in range(i + 1):
            if (i, j) != (1, 1):
                packed_ref[at : at + TILE] = block(i, j)
                at += TILE
    diagonal = jnp.sum(block(1, 1) * eye(TILE), axis=0, keepdims=True)
    packed_ref[at:] = jnp.broadcast_to(diagonal, (SUB, TILE))
    copies = [
        pltpu.make_async_copy(packed_ref, out_ref.at[k], sems.at[k])
        for k in range(out_ref.shape[0])
    ]
    for copy in copies:
        copy.start()
    for copy in copies:
        copy.wait()


def side_body(index_ref, rows_ref, *refs):
    piece_refs, full_ref = refs[:-1], refs[-1]
    width = full_ref.shape[0]
    columns = piece_refs[0].shape[0]
    mid = cluster_rows(rows_ref, 1)
    full_ref[:, :width] = summed_gram(cluster_rows(rows_ref, 0), mid)
    full_ref[:, width:] = summed_gram(cluster_rows(rows_ref, 2), mid)
    for k, piece_ref in enumerate(piece_refs):
        at = lax.rem(index_ref[0] + k, len(piece_refs))
        piece_ref[...] = full_ref[pl.ds(pl.multiple_of(at * columns, 8), columns), :]


def last_body(rows_ref, out_ref):
    last = cluster_rows(rows_ref, 2)
    out_ref[...] = summed_gram(last, last)


def even_body(rows_ref, carried_ref, out_ref):
    width = carried_ref.shape[0]
    first, last = cluster_rows(rows_ref, 0), cluster_rows(rows_ref, 2)
    out_ref[:, :width] = summed_gram(first, first) + carried_ref[...]
    out_ref[:, width:] = summed_gram(last, first)


def eye(n):
    rows = lax.broadcasted_iota(jnp.int32, (n, n), 0)
    return jnp.where(rows == lax.broadcasted_iota(jnp.int32, (n, n), 1), 1.0, 0.0).astype(F32)


def factor_tile(a_ref, w_ref, panel):
    n = a_ref.shape[0]
    tiles = panel // SUB
    row = lax.broadcasted_iota(jnp.int32, (SUB, n), 0)

    def splat(value, r):
        return jnp.broadcast_to(value[r : r + 1, :], (SUB, n))

    for b in range(0, n, panel):
        pa = [a_ref[b + t * SUB : b + (t + 1) * SUB, :] for t in range(tiles)]
        pw = [w_ref[b + t * SUB : b + (t + 1) * SUB, :] for t in range(tiles)]
        for top in range(tiles):
            at = b + top * SUB
            cols = [
                {t: jnp.broadcast_to(pa[t][:, at + k : at + k + 1], (SUB, n)) for t in range(top, tiles)}
                for k in range(SUB)
            ]
            scale = jnp.ones((SUB, n), F32)
            for r in range(0, SUB, 2):
                p = splat(cols[r][top], r)
                q = splat(cols[r][top], r + 1)
                c = splat(cols[r + 1][top], r + 1)
                over = 1.0 / (p * c - q * q)
                g0, g1, g2 = c * over, q * over, p * over
                h = q * (1.0 / p)
                scale = jnp.where(row == r, p, jnp.where(row == r + 1, c - q * h, scale))
                first = top if r + 2 < SUB else top + 1
                m0, m1 = {}, {}
                for t in range(first, tiles):
                    c0, c1 = cols[r][t], cols[r + 1][t]
                    m0[t] = c0 * g0 - c1 * g1
                    m1[t] = c1 * g2 - c0 * g1
                    if t == top:
                        m0[t] = jnp.where(row > r + 1, m0[t], 0.0)
                        m1[t] = jnp.where(row > r + 1, m1[t], 0.0)
                for k in range(r + 2, SUB):
                    s0, s1 = splat(cols[k][top], r), splat(cols[k][top], r + 1)
                    for t in range(first, tiles):
                        cols[k][t] = cols[k][t] - m0[t] * s0 - m1[t] * s1
                for x in (pa, pw):
                    s0, s1 = splat(x[top], r), splat(x[top], r + 1)
                    for t in range(first, tiles):
                        x[t] = x[t] - m0[t] * s0 - m1[t] * s1
                    x[top] = jnp.where(row == r + 1, x[top] - h * s0, x[top])
            rs = lax.rsqrt(scale)
            pa[top] = pa[top] * rs
            pw[top] = pw[top] * rs
        left = jnp.concatenate(pa, axis=0)
        right = jnp.concatenate(pw, axis=0)
        w_ref[b : b + panel, :] = right
        if b + panel < n:
            u = mm(left, jnp.concatenate([left, right], axis=1), TN, HI)
            a_ref[b + panel :, :] = a_ref[b + panel :, :] - u[b + panel :, :n]
            w_ref[b + panel :, :] = w_ref[b + panel :, :] - u[b + panel :, n:]


def summed(ref, at, rows):
    value = ref[0, at : at + rows]
    for k in range(1, ref.shape[0]):
        value = value + ref[k, at : at + rows]
    return value


def factor_body(blocks_ref, damping_ref, out_ref, a_ref, w_ref):
    n = TILE
    count = damping_ref.shape[1] // n
    packed = summed(blocks_ref, 0, n)
    turned_over = packed.T
    row = lax.broadcasted_iota(jnp.int32, (n, n), 0)
    col = lax.broadcasted_iota(jnp.int32, (n, n), 1)
    at, s = n, [[jnp.where(row >= col, packed, turned_over)]]
    for i in range(1, count):
        s.append([])
        for j in range(i + 1):
            if (i, j) != (1, 1):
                s[i].append(summed(blocks_ref, at, n))
                at += n
            else:
                s[i].append(jnp.where(row < col, packed, turned_over))
    diagonal = summed(blocks_ref, at, SUB)[:1]
    s[1][1] = jnp.where(row == col, diagonal, s[1][1])
    for i in range(count):
        s[i][i] = s[i][i] + eye(n) * damping_ref[:, i * n : (i + 1) * n]
    for d in range(count - 1):
        a_ref[...] = s[d][d]
        w_ref[...] = eye(n)
        factor_tile(a_ref, w_ref, 64)
        w = w_ref[...]
        out_ref[(d * (d + 1) // 2 + d) * n : (d * (d + 1) // 2 + d + 1) * n] = w
        for i in range(d + 1, count):
            s[i][d] = mm(s[i][d], w, NT, HI)
            out_ref[(i * (i + 1) // 2 + d) * n : (i * (i + 1) // 2 + d + 1) * n] = s[i][d]
        for i in range(d + 1, count):
            for k in range(d + 1, i + 1):
                s[i][k] = s[i][k] - mm(s[i][d], s[k][d], NT, HI)
    out_ref[-n:] = s[-1][-1]


def solve_body(factor_ref, *refs):
    right_refs, (low_ref, high_ref, a_ref, w_ref) = refs[:-4], refs[-4:]
    n = TILE
    rows, width = right_refs[0].shape[0], right_refs[0].shape[1] // 2
    count = width // n
    block = lambda i, j: factor_ref[(i * (i + 1) // 2 + j) * n : (i * (i + 1) // 2 + j + 1) * n]
    a_ref[...] = block(count - 1, count - 1)
    w_ref[...] = eye(n)
    right = right_refs[0][...]
    for ref in right_refs[1:]:
        right = right + ref[...]
    right = jnp.concatenate([right[:, :width], right[:, width:]], axis=0)
    done = []
    for i in range(count):
        part = right[:, i * n : (i + 1) * n]
        for j in range(i):
            part = part - mm(done[j], block(i, j), NT, HI)
        if i == count - 1:
            factor_tile(a_ref, w_ref, 64)
            inverse = w_ref[...]
        else:
            inverse = block(i, i)
        done.append(mm(part, inverse, NT, HI))
        for k in range(low_ref.shape[0]):
            low_ref[k, :, i * n : (i + 1) * n] = done[i][:rows]
        high_ref[:, i * n : (i + 1) * n] = done[i][rows:]


def whole(ref):
    return jnp.concatenate([ref[k] for k in range(ref.shape[0])], axis=0)


def total_body(parts_ref, out_ref):
    value = parts_ref[0]
    for k in range(1, parts_ref.shape[0]):
        value = value + parts_ref[k]
    out_ref[...] = value


def high_body(y_ref, mine_ref, out_ref):
    out_ref[...] = mm(mine_ref[...], whole(y_ref), NT, HI)


def low_body(y_ref, low_mine_ref, high_mine_ref, even_ref, diag_ref, pair_ref):
    columns, width = diag_ref.shape
    mine = jnp.concatenate([low_mine_ref[0], high_mine_ref[...]], axis=0)
    u = mm(mine, whole(y_ref), NT, HI)
    diag_ref[...] = even_ref[:, :width] - u[:columns]
    pair_ref[...] = even_ref[:, width:] - u[columns:]


def exchanged(value, axis):
    return lax.all_to_all(value, axis, 0, 0, tiled=True)


def turned(value, axis, by):
    if by == 0:
        return value
    devices = lax.axis_size(axis)
    return lax.ppermute(value, axis, [(i, (i + by) % devices) for i in range(devices)])


def after(value, other):
    return lax.optimization_barrier((value, other))[0]


def shape(*dims):
    return jax.ShapeDtypeStruct(dims, F32)


def local(jacobian, owner, damping):
    points, _, _, width = jacobian.shape
    owners = lax.axis_size(PTS)
    groups = lax.axis_size("grp")
    columns = width // groups
    capacity = max(2, 2 * points // owners)
    rows = jnp.transpose(jacobian, (1, 2, 0, 3))
    segment = owner.reshape(1, points)
    tiles = (width // TILE) * (width // TILE + 1) // 2

    sent = call(
        lambda *refs: pack_body(capacity, *refs),
        jax.ShapeDtypeStruct((owners, capacity, 9 * width), BF16),
        segment,
        rows,
    )
    got = exchanged(sent, PTS)
    packed = (tiles - 1) * TILE + SUB
    odd = pl.pallas_call(
        odd_body,
        out_shape=shape(groups, packed, TILE),
        in_specs=[pl.BlockSpec(memory_space=pltpu.VMEM)],
        out_specs=pl.BlockSpec(memory_space=pltpu.HBM),
        scratch_shapes=[pltpu.VMEM((packed, TILE), F32), pltpu.SemaphoreType.DMA((groups,))],
        compiler_params=PARAMS,
        cost_estimate=cost(10**9, 10**6),
    )(got)
    odd = exchanged(odd, "grp")
    last = call(last_body, shape(width, width), got, cost=cost(10**9, 10**6))
    carried = turned(last, PTS, 1)
    index = lax.axis_index("grp").astype(jnp.int32).reshape(1)
    side = call(
        side_body,
        [shape(columns, 2 * width)] * groups,
        index,
        got,
        cost=cost(10**9, 10**6),
        scratch=[pltpu.VMEM((width, 2 * width), F32)],
        scalars=1,
    )
    side = [turned(piece, "grp", k) for k, piece in enumerate(side)]
    even = call(even_body, shape(width, 2 * width), got, carried, cost=cost(10**9, 10**6))
    even = exchanged(after(even, odd).reshape(groups, columns, 2 * width), "grp")
    factor = call(
        factor_body,
        shape(tiles * TILE, TILE),
        odd,
        damping,
        cost=cost(10**10, 10**6),
        scratch=[pltpu.VMEM((TILE, TILE), F32)] * 2,
    )
    low_mine, high_mine = call(
        solve_body,
        [shape(groups, columns, width), shape(columns, width)],
        factor,
        *side,
        cost=cost(3 * 10**9, 10**6),
        scratch=[pltpu.VMEM((TILE, TILE), F32)] * 2,
    )
    y_high = lax.all_gather(high_mine, "grp", axis=0, tiled=False)
    high = call(high_body, shape(columns, width), y_high, high_mine)
    low_mine, high, even = lax.optimization_barrier((low_mine, high, even))
    high = turned(high, PTS, 1)
    y_low = exchanged(low_mine, "grp")
    even = call(total_body, shape(columns, 2 * width), even)
    diag, pair = call(
        low_body, [shape(columns, width)] * 2, y_low, low_mine, high_mine, even
    )
    return ((diag - high).T[None], pair.T[None])


def solution(mesh):
    torus = Mesh(
        mesh.devices.reshape(8, 8, 2, mesh.shape["grp"]), ("pts_0", "pts_1", "pts_2", "grp")
    )
    placed = (P(PTS_GRP, None, None, None), P(PTS_GRP, None), P(PTS, None))
    return jax.shard_map(
        local,
        mesh=torus,
        in_specs=placed,
        out_specs=(P(PTS, None, "grp"), P(PTS, None, "grp")),
        check_vma=False,
    )
```
